256 devices in a mesh: freq: 16 (over y_lo, x, core), blk: 16 (over y_hi, z).
Axes of the slice: x: 4, y: 4 (y_hi: 2, y_lo: 2; y = y_hi * 2 + y_lo), z: 8, core: 2. Of those that a mesh axis runs over, the one named last changes fastest.
Arguments:
- samples: bfloat16 [16, 128, 69376], P('blk', 'freq'), may hold values from -6 to 6
- chan_list: int32 [128], replicated, may hold values from 0 to 128, as said below
Outputs:
- visibilities: bfloat16 [128, 16, 9, 2, 128, 128], P('freq', 'blk')
The draws below stay inside these ranges and needn't reach their ends.
Inputs may be any that keep to these rules, and one draw needn't show every extreme that they name: `chan_list`: 128 distinct bins in increasing order, the first 0 and the last 128.
All inputs are finite; a program needn't handle non-finite values.
Results may differ from the reference program's by a relative error of at most 0.0065.
Values may be sent and summed in bfloat16 or wider, within the bound.
No kernel may reach another device: no remote copies, remote signals or barrier semaphores. Data moves between devices by JAX's collectives and lax.ppermute only.
A program may use at most 64 MiB of HBM per device.

```python
import jax
import jax.numpy as jnp
from jax import lax

POINTS = 256
TAPS = 16
CHANNELS = 128
SPECTRA = 256
BLOCKS = 16
TILE = 128
OFFSETS = 9
SAMPLES = 69376


def draw_chan_list(key, part):
    interior = jax.random.permutation(key, POINTS // 2 - 1).astype(jnp.int32) + 1
    picked = jnp.sort(interior[:CHANNELS - 2]).astype(jnp.int32)
    first_bin = jnp.zeros((1,), jnp.int32)
    last_bin = jnp.full((1,), POINTS // 2, jnp.int32)
    return jnp.concatenate([first_bin, picked, last_bin]).astype(jnp.int32)


def block_levels(stream_key, shape, cuts, low, high):
    gain, own = 1.0, jax.random.fold_in(stream_key, 6)
    for axis_at, blocks in cuts:
        heights = jnp.exp(jax.random.uniform(jax.random.fold_in(own, axis_at), (blocks,), jnp.float32, low / len(cuts), high / len(cuts)))
        gain = gain * jnp.repeat(heights, shape[axis_at] // blocks).reshape([-1 if axis == axis_at else 1 for axis in range(len(shape))])
    return gain


def scatter_about(own_key, dims, spread, reach, shards=(), held_as=jnp.bfloat16):
    entries = spread * jax.random.normal(own_key, dims, jnp.float32)
    if shards:
        entries = entries * block_levels(own_key, dims, shards, -0.22, 0.18)
    return jnp.clip(entries, -reach, reach).astype(held_as)


def setup_inputs(seed: int = 0) -> dict:
    key_list = jax.random.split(jax.random.key(seed), 3)
    samples = scatter_about(key_list[0], (BLOCKS, TILE, SAMPLES), 1.0, 6.0, ((0, 16), (1, 16)))
    chan_list = draw_chan_list(jax.random.fold_in(key_list[2], 71), 0)
    return dict(samples=samples, chan_list=chan_list)


def filter_table(chan_list):
    window_len = TAPS * POINTS
    position = jnp.arange(window_len, dtype=jnp.float32)
    offset_pos = (position - window_len / 2 + 0.5) / POINTS
    taper = 0.5 - 0.5 * jnp.cos(2.0 * jnp.pi * (position + 0.5) / window_len)
    window = jnp.sin(jnp.pi * offset_pos) / (jnp.pi * offset_pos) * taper
    window = window / jnp.sqrt(jnp.sum(window * window))
    window = window.reshape(TAPS, POINTS)
    columns = jnp.arange(POINTS, dtype=jnp.int32)
    angles = (chan_list.astype(jnp.int32)[:, None] * columns[None, :] % POINTS).astype(jnp.float32) * (2.0 * jnp.pi / POINTS)
    cosines = window[:, None, :] * jnp.cos(angles)[None, :, :]
    sine_part = -window[:, None, :] * jnp.sin(angles)[None, :, :]
    return jnp.concatenate([cosines, sine_part], axis=1).astype(jnp.bfloat16)

def reference(samples, chan_list):
    filters = filter_table(chan_list).astype(jnp.float32)
    frames = samples.reshape(BLOCKS * TILE, SPECTRA + TAPS - 1, POINTS)
    running = jnp.zeros((2 * CHANNELS, BLOCKS * TILE, SPECTRA), jnp.float32)
    for tap_index in range(TAPS):
        segment = frames[:, tap_index:tap_index + SPECTRA].astype(jnp.float32)
        running = running + jnp.einsum('kn,isn->kis', filters[tap_index], segment, precision=lax.Precision.HIGHEST)
    voltages = running.astype(jnp.bfloat16).reshape(2, CHANNELS, BLOCKS, TILE, SPECTRA)

    def one_block(block_idx):
        own_tile = lax.dynamic_index_in_dim(voltages, block_idx, 2, keepdims=False).astype(jnp.float32)
        blocks_out = []
        for offset_idx in range(OFFSETS):
            source = ((block_idx - offset_idx + BLOCKS) % BLOCKS).astype(jnp.int32)
            other = lax.dynamic_index_in_dim(voltages, source, 2, keepdims=False).astype(jnp.float32)
            real_part = jnp.einsum('pcis,pcjs->cij', own_tile, other, precision=lax.Precision.HIGHEST)
            imag_part = jnp.einsum('cis,cjs->cij', own_tile[1], other[0], precision=lax.Precision.HIGHEST) - jnp.einsum('cis,cjs->cij', own_tile[0], other[1], precision=lax.Precision.HIGHEST)
            blocks_out.append(jnp.stack([real_part, imag_part], axis=1) * (1.0 / SPECTRA))
        return jnp.stack(blocks_out, axis=1).astype(jnp.bfloat16)
    stacked = lax.map(one_block, jnp.arange(BLOCKS, dtype=jnp.int32))
    return jnp.transpose(stacked, (1, 0, 2, 3, 4, 5))
```

```python
import jax
import jax.numpy as jnp
from jax import lax
from jax.sharding import PartitionSpec as P

POINTS = 256
TAPS = 16
CHANNELS = 128
SPECTRA = 256
CHUNKS = 2


def shifted(value, steps):
    count = lax.axis_size("blk")
    return lax.ppermute(value, "blk", [(b, (b + steps) % count) for b in range(count)])


def filter_tables(chan_list, freq_size):
    window_len = TAPS * POINTS
    position = jnp.arange(window_len, dtype=jnp.float32)
    offset_pos = (position - window_len / 2 + 0.5) / POINTS
    taper = 0.5 - 0.5 * jnp.cos(2.0 * jnp.pi * (position + 0.5) / window_len)
    window = jnp.sin(jnp.pi * offset_pos) / (jnp.pi * offset_pos) * taper
    window = window / jnp.sqrt(jnp.sum(window * window))
    window = window.reshape(TAPS, 1, POINTS)
    columns = jnp.arange(POINTS, dtype=jnp.int32)
    angles = (chan_list[:, None] * columns[None, :] % POINTS).astype(jnp.float32) * (
        2.0 * jnp.pi / POINTS
    )
    waves = jnp.stack([jnp.cos(angles), -jnp.sin(angles)], axis=0)
    waves = waves.reshape(2, freq_size, CHUNKS, -1, POINTS).transpose(2, 1, 0, 3, 4)
    return [
        (window * waves[chunk].reshape(1, -1, POINTS)).astype(jnp.bfloat16)
        for chunk in range(CHUNKS)
    ]


def channelize(frames, filters):
    return lax.conv_general_dilated(
        frames,
        filters,
        window_strides=(1,),
        padding="VALID",
        dimension_numbers=("NWC", "WOI", "CNW"),
        preferred_element_type=jnp.float32,
    ).astype(jnp.bfloat16)


def cross_block(stacked, moving):
    product = lax.dot_general(
        stacked, moving, (((0, 3), (0, 3)), ((1,), (1,))), preferred_element_type=jnp.float32
    )
    chan_count, _, tile = product.shape
    return (product * (1.0 / SPECTRA)).astype(jnp.bfloat16).reshape(chan_count, 2, tile, tile)


def stack_parts(own):
    return jnp.stack(
        [
            jnp.concatenate([own[0], own[1]], axis=1),
            jnp.concatenate([own[1], -own[0]], axis=1),
        ]
    )


def body(samples, chan_list):
    freq_size = lax.axis_size("freq")
    inputs = samples.shape[1]
    frames = samples.reshape(inputs, samples.shape[2] // POINTS, POINTS)
    tables = filter_tables(chan_list, freq_size)
    chans = CHANNELS // freq_size // CHUNKS

    turned = []
    for chunk in range(CHUNKS):
        voltages = channelize(frames, tables[chunk])
        sectioned = voltages.reshape(freq_size, 2, chans, inputs, SPECTRA)
        turned.append(
            lax.all_to_all(sectioned, "freq", split_axis=0, concat_axis=3, tiled=True).reshape(
                2, chans, freq_size * inputs, SPECTRA
            )
        )
    half = lax.axis_size("blk") // 2
    rows = []
    for chunk in range(CHUNKS):
        own = turned[chunk]
        stacked = stack_parts(own)
        blocks = [None] * (half + 1)
        blocks[0] = own
        ups = half // 2 if chunk % 2 == 0 else half // 2 - 1
        for offset in range(1, ups + 1):
            blocks[offset] = shifted(blocks[offset - 1], 1)
        blocks[half - 1] = shifted(own, half - 1)
        for offset in range(half - 2, ups, -1):
            blocks[offset] = shifted(blocks[offset + 1], -1)
        blocks[half] = shifted(own, half)
        rows.append(jnp.stack([cross_block(stacked, block) for block in blocks], axis=1))
    return jnp.concatenate(rows, axis=0)[:, None]


def solution(mesh):
    in_specs = (P("blk", "freq", None), P())
    out_specs = P("freq", "blk", None, None, None, None)
    return jax.shard_map(body, mesh=mesh, in_specs=in_specs, out_specs=out_specs, check_vma=False)
```

```python
import jax
import jax.numpy as jnp
from jax import lax
from jax.sharding import PartitionSpec as P

POINTS = 256
TAPS = 16
CHANNELS = 128
SPECTRA = 256


def along_ring(value, steps, other=0):
    half = lax.axis_size("blk") // 2
    pairs = []
    for b in range(2 * half):
        column, plane = b // half, b % half
        pairs.append((b, (column + other) % 2 * half + (plane + steps) % half))
    return lax.ppermute(value, "blk", pairs)


def to_twin(value):
    return along_ring(value, 0, 1)


def filter_table(chan_list, freq_size):
    window_len = TAPS * POINTS
    position = jnp.arange(window_len, dtype=jnp.float32)
    offset_pos = (position - window_len / 2 + 0.5) / POINTS
    taper = 0.5 - 0.5 * jnp.cos(2.0 * jnp.pi * (position + 0.5) / window_len)
    window = jnp.sin(jnp.pi * offset_pos) / (jnp.pi * offset_pos) * taper
    window = window / jnp.sqrt(jnp.sum(window * window))
    window = window.reshape(TAPS, 1, POINTS)
    columns = jnp.arange(POINTS, dtype=jnp.int32)
    angles = (chan_list[:, None] * columns[None, :] % POINTS).astype(jnp.float32) * (
        2.0 * jnp.pi / POINTS
    )
    waves = jnp.stack([jnp.cos(angles), -jnp.sin(angles)], axis=0)
    waves = waves.reshape(2, freq_size, 2, -1, POINTS).transpose(2, 1, 0, 3, 4)
    return (window * waves.reshape(1, -1, POINTS)).astype(jnp.bfloat16)


def channelize(frames, filters):
    return lax.conv_general_dilated(
        frames,
        filters,
        window_strides=(1,),
        padding="VALID",
        dimension_numbers=("NWC", "WOI", "CNW"),
        preferred_element_type=jnp.float32,
    ).astype(jnp.bfloat16)


def cross_block(stacked, moving):
    product = lax.dot_general(
        stacked, moving, (((0, 3), (0, 3)), ((1,), (1,))), preferred_element_type=jnp.float32
    )
    chan_count, _, tile = product.shape
    return (product * (1.0 / SPECTRA)).astype(jnp.bfloat16).reshape(chan_count, 2, tile, tile)


def stack_parts(own):
    return jnp.stack(
        [
            jnp.concatenate([own[0], own[1]], axis=1),
            jnp.concatenate([own[1], -own[0]], axis=1),
        ]
    )


def body(samples, chan_list):
    freq_size = lax.axis_size("freq")
    half = lax.axis_size("blk") // 2
    column, plane = lax.axis_index("blk") // half, lax.axis_index("blk") % half
    inputs = samples.shape[1]
    tile = freq_size * inputs
    frames = samples.reshape(inputs, samples.shape[2] // POINTS, POINTS)
    chans = CHANNELS // freq_size // 2
    voltages = channelize(frames, filter_table(chan_list, freq_size))
    voltages = voltages.reshape(2, freq_size, 2, 1, chans, inputs, SPECTRA)

    kept = lax.dynamic_index_in_dim(voltages, column, 0, keepdims=False)
    given = lax.dynamic_index_in_dim(voltages, 1 - column, 0, keepdims=False)
    pair = jnp.concatenate([kept, to_twin(given)], axis=2)
    pair = lax.all_to_all(pair, "freq", split_axis=0, concat_axis=4, tiled=True)
    lower, upper = slice(0, chans // 2), slice(chans // 2, chans)

    blocks = {0: pair.reshape(2, 2, chans, tile, SPECTRA)}
    tiles = {}

    def cross(owner, partner, where):
        own, moving = blocks[owner][:, :, where], blocks[partner][:, :, where]
        swap = (plane + partner) % half > (plane + owner) % half
        return [
            cross_block(
                stack_parts(own[:, block]),
                jnp.where(swap, moving[:, 1 - block], moving[:, block]),
            )
            for block in range(2)
        ]

    def near_tiles(partners):
        made = [cross(0, partner, where) for partner, where in partners]
        moved = to_twin(jnp.stack([both[1] for both in made]))
        for index, (partner, where) in enumerate(partners):
            tiles[-partner % half, where.start] = (made[index][0], moved[index])

    def far_tiles(owner, partner, where):
        both = cross(owner, partner, where)
        tiles[(owner - partner) % half, where.start] = (
            along_ring(both[0], owner),
            along_ring(both[1], owner, 1),
        )

    def step(partner, where=slice(None)):
        way = 1 if partner < 0 else -1
        blocks[partner] = along_ring(blocks[partner + way][:, :, where], way)

    def settle():
        nonlocal tiles, blocks
        tiles, blocks = lax.optimization_barrier((tiles, blocks))

    every = slice(0, chans)
    step(-1), step(1)
    own = blocks[0]
    made = [
        cross_block(stack_parts(own[:, i]), own[:, i ^ other]) for other in range(2) for i in range(2)
    ]
    moved = to_twin(jnp.stack([made[1], made[3]]))
    tiles[0, 0], tiles[half, 0] = (made[0], moved[0]), (made[2], moved[1])
    settle()
    step(-2), step(2)
    near_tiles([(-1, every), (1, every)])
    settle()
    step(-3, lower), step(3, upper)
    far_tiles(-1, 2, lower), far_tiles(1, -2, upper)
    near_tiles([(-2, every), (2, every)])
    settle()
    blocks[-3] = jnp.concatenate([blocks[-3], blocks[-3]], axis=2)
    blocks[3] = jnp.concatenate([blocks[3], blocks[3]], axis=2)
    far_tiles(1, -3, lower), far_tiles(-1, 3, upper)
    near_tiles([(-3, lower), (3, upper)])

    def whole(place):
        found = []
        for offset in range(half + 1):
            parts = [tiles[key][place] for key in sorted(tiles) if key[0] == offset]
            found.append(parts[0] if len(parts) == 1 else jnp.concatenate(parts, axis=0))
        return jnp.stack(found, axis=1)

    mine, theirs = whole(0), whole(1)
    low = jnp.where(column == 0, mine, theirs)
    high = jnp.where(column == 0, theirs, mine)
    return jnp.concatenate([low, high], axis=0)[:, None]


def solution(mesh):
    in_specs = (P("blk", "freq", None), P())
    out_specs = P("freq", "blk", None, None, None, None)
    return jax.shard_map(body, mesh=mesh, in_specs=in_specs, out_specs=out_specs, check_vma=False)
```

```python
import jax
import jax.numpy as jnp
from jax import lax
from jax.experimental import pallas as pl
from jax.experimental.pallas import tpu as pltpu
from jax.sharding import PartitionSpec as P

POINTS = 256
TAPS = 16
CHANNELS = 128
SPECTRA = 256


def along_ring(value, steps, other=0):
    half = lax.axis_size("blk") // 2
    pairs = []
    for b in range(2 * half):
        column, plane = b // half, b % half
        pairs.append((b, (column + other) % 2 * half + (plane + steps) % half))
    return lax.ppermute(value, "blk", pairs)


def to_twin(value):
    return along_ring(value, 0, 1)


def filter_table(chan_list, freq_size):
    window_len = TAPS * POINTS
    position = jnp.arange(window_len, dtype=jnp.float32)
    offset_pos = (position - window_len / 2 + 0.5) / POINTS
    taper = 0.5 - 0.5 * jnp.cos(2.0 * jnp.pi * (position + 0.5) / window_len)
    window = jnp.sin(jnp.pi * offset_pos) / (jnp.pi * offset_pos) * taper
    window = window / jnp.sqrt(jnp.sum(window * window))
    window = window.reshape(TAPS, 1, POINTS)
    columns = jnp.arange(POINTS, dtype=jnp.int32)
    angles = (chan_list[:, None] * columns[None, :] % POINTS).astype(jnp.float32) * (
        2.0 * jnp.pi / POINTS
    )
    waves = jnp.stack([jnp.cos(angles), -jnp.sin(angles)], axis=0)
    waves = waves.reshape(2, freq_size, 2, -1, POINTS).transpose(2, 1, 0, 3, 4)
    return (window * waves.reshape(1, -1, POINTS)).astype(jnp.bfloat16)


def channelize(frames, filters):
    return lax.conv_general_dilated(
        frames,
        filters,
        window_strides=(1,),
        padding="VALID",
        dimension_numbers=("NWC", "WOI", "CNW"),
        preferred_element_type=jnp.float32,
    ).astype(jnp.bfloat16)


def visibility_kernel(swaps, own, *refs):
    partners, (kept, given) = refs[:-2], refs[-2:]
    for block in range(2):
        real, imag = own[0, block, 0], own[1, block, 0]
        stacked = jnp.concatenate(
            [
                jnp.concatenate([real, imag], axis=1),
                jnp.concatenate([imag, -real], axis=1),
            ],
            axis=0,
        )
        tile = real.shape[0]
        found = kept if block == 0 else given
        for index, partner in enumerate(partners):
            other = swaps[index] if block == 0 else 1 - swaps[index]
            moving = jnp.concatenate([partner[0, other, 0], partner[1, other, 0]], axis=1)
            product = lax.dot_general(
                stacked, moving, (((1,), (1,)), ((), ())), preferred_element_type=jnp.float32
            )
            product = (product * (1.0 / SPECTRA)).astype(jnp.bfloat16)
            found[index, 0, 0] = product[:tile]
            found[index, 0, 1] = product[tile:]


def visibilities(own, partners, swaps):
    _, _, chans, tile, spectra = own.shape
    count = len(partners)
    data = pl.BlockSpec((2, 2, 1, tile, spectra), lambda chan, _: (0, 0, chan, 0, 0))
    made = pl.BlockSpec((count, 1, 2, tile, tile), lambda chan, _: (0, chan, 0, 0, 0))
    shape = jax.ShapeDtypeStruct((count, chans, 2, tile, tile), jnp.bfloat16)
    return pl.pallas_call(
        visibility_kernel,
        grid_spec=pltpu.PrefetchScalarGridSpec(
            num_scalar_prefetch=1,
            grid=(chans,),
            in_specs=[data] * (1 + count),
            out_specs=[made, made],
        ),
        out_shape=[shape, shape],
        compiler_params=pltpu.CompilerParams(vmem_limit_bytes=24 * 1024 * 1024),
    )(jnp.stack(swaps).astype(jnp.int32), own, *partners)


def body(samples, chan_list):
    freq_size = lax.axis_size("freq")
    half = lax.axis_size("blk") // 2
    column, plane = lax.axis_index("blk") // half, lax.axis_index("blk") % half
    inputs = samples.shape[1]
    tile = freq_size * inputs
    frames = samples.reshape(inputs, samples.shape[2] // POINTS, POINTS)
    chans = CHANNELS // freq_size // 2
    voltages = channelize(frames, filter_table(chan_list, freq_size))
    voltages = voltages.reshape(2, freq_size, 2, 1, chans, inputs, SPECTRA)

    kept = lax.dynamic_index_in_dim(voltages, column, 0, keepdims=False)
    given = lax.dynamic_index_in_dim(voltages, 1 - column, 0, keepdims=False)
    pair = jnp.concatenate([kept, to_twin(given)], axis=2)
    pair = lax.all_to_all(pair, "freq", split_axis=0, concat_axis=4, tiled=True)

    blocks, tiles = {0: pair.reshape(2, 2, chans, tile, SPECTRA)}, {}

    def near(*partners):
        sources = [blocks[0 if at == half else at] for at in partners]
        swaps = [
            jnp.bool_(True) if at == half else (plane + at) % half > plane for at in partners
        ]
        mine, theirs = visibilities(blocks[0], sources, swaps)
        moved = to_twin(theirs)
        for index, at in enumerate(partners):
            tiles[half if at == half else -at % half] = (mine[index], moved[index])

    def far(owner, partner):
        swap = (plane + partner) % half > (plane + owner) % half
        mine, theirs = visibilities(blocks[owner], [blocks[partner]], [swap])
        tiles[(owner - partner) % half] = (
            along_ring(mine, owner)[0],
            along_ring(theirs, owner, 1)[0],
        )

    def step(partner):
        way = 1 if partner < 0 else -1
        blocks[partner] = along_ring(blocks[partner + way], way)

    def settle():
        nonlocal tiles, blocks
        tiles, blocks = lax.optimization_barrier((tiles, blocks))

    step(-1), step(1)
    near(0, half)
    settle()
    step(-2), step(2)
    near(-1, 1)
    settle()
    step(-3)
    near(-2, 2)
    far(-1, 2)
    settle()
    far(1, -3)
    near(-3)

    def whole(place):
        return jnp.stack([tiles[offset][place] for offset in range(half + 1)], axis=1)

    mine, theirs = whole(0), whole(1)
    low = jnp.where(column == 0, mine, theirs)
    high = jnp.where(column == 0, theirs, mine)
    return jnp.concatenate([low, high], axis=0)[:, None]


def solution(mesh):
    in_specs = (P("blk", "freq", None), P())
    out_specs = P("freq", "blk", None, None, None, None)
    return jax.shard_map(body, mesh=mesh, in_specs=in_specs, out_specs=out_specs, check_vma=False)
```

```python
import jax
import jax.numpy as jnp
from jax import lax
from jax.experimental import pallas as pl
from jax.experimental.pallas import tpu as pltpu
from jax.sharding import Mesh
from jax.sharding import PartitionSpec as P

POINTS = 256
TAPS = 16
CHANNELS = 128
SPECTRA = 256


def along_ring(value, steps, other=0):
    half = lax.axis_size("plane")
    pairs = []
    for b in range(2 * half):
        column, plane = b // half, b % half
        pairs.append((b, (column + other) % 2 * half + (plane + steps) % half))
    return lax.ppermute(value, ("column", "plane"), pairs)


def to_twin(value):
    return along_ring(value, 0, 1)


def filter_table(chan_list, freq_size):
    window_len = TAPS * POINTS
    position = jnp.arange(window_len, dtype=jnp.float32)
    offset_pos = (position - window_len / 2 + 0.5) / POINTS
    taper = 0.5 - 0.5 * jnp.cos(2.0 * jnp.pi * (position + 0.5) / window_len)
    window = jnp.sin(jnp.pi * offset_pos) / (jnp.pi * offset_pos) * taper
    window = window / jnp.sqrt(jnp.sum(window * window))
    window = window.reshape(TAPS, 1, POINTS)
    columns = jnp.arange(POINTS, dtype=jnp.int32)
    angles = (chan_list[:, None] * columns[None, :] % POINTS).astype(jnp.float32) * (
        2.0 * jnp.pi / POINTS
    )
    waves = jnp.stack([jnp.cos(angles), -jnp.sin(angles)], axis=0)
    waves = waves.reshape(2, freq_size, 2, -1, POINTS).transpose(1, 2, 0, 3, 4)
    return (window * waves.reshape(1, -1, POINTS)).astype(jnp.bfloat16)


def channelize(frames, filters):
    return lax.conv_general_dilated(
        frames,
        filters,
        window_strides=(1,),
        padding="VALID",
        dimension_numbers=("NWC", "WOI", "CNW"),
        preferred_element_type=jnp.float32,
    ).astype(jnp.bfloat16)


def visibility_kernel(swaps, own, *refs):
    partners, (kept, given) = refs[:-2], refs[-2:]
    for block in range(2):
        real, imag = own[0, block, 0], own[1, block, 0]
        stacked = jnp.concatenate(
            [
                jnp.concatenate([real, imag], axis=1),
                jnp.concatenate([imag, -real], axis=1),
            ],
            axis=0,
        )
        tile = real.shape[0]
        found = kept if block == 0 else given
        for index, partner in enumerate(partners):
            other = swaps[index] if block == 0 else 1 - swaps[index]
            moving = jnp.concatenate([partner[0, other, 0], partner[1, other, 0]], axis=1)
            product = lax.dot_general(
                stacked, moving, (((1,), (1,)), ((), ())), preferred_element_type=jnp.float32
            )
            product = (product * (1.0 / SPECTRA)).astype(jnp.bfloat16)
            found[index, 0, 0] = product[:tile]
            found[index, 0, 1] = product[tile:]


def visibilities(own, partners, swaps):
    _, _, chans, tile, spectra = own.shape
    count = len(partners)
    data = pl.BlockSpec((2, 2, 1, tile, spectra), lambda chan, _: (0, 0, chan, 0, 0))
    made = pl.BlockSpec((count, 1, 2, tile, tile), lambda chan, _: (0, chan, 0, 0, 0))
    shape = jax.ShapeDtypeStruct((count, chans, 2, tile, tile), jnp.bfloat16)
    return pl.pallas_call(
        visibility_kernel,
        grid_spec=pltpu.PrefetchScalarGridSpec(
            num_scalar_prefetch=1,
            grid=(chans,),
            in_specs=[data] * (1 + count),
            out_specs=[made, made],
        ),
        out_shape=[shape, shape],
        compiler_params=pltpu.CompilerParams(vmem_limit_bytes=24 * 1024 * 1024),
    )(jnp.stack(swaps).astype(jnp.int32), own, *partners)


def body(samples, chan_list):
    freq_size = lax.axis_size("freq")
    half = lax.axis_size("plane")
    column, plane = lax.axis_index("column"), lax.axis_index("plane")
    inputs = samples.shape[1]
    tile = freq_size * inputs
    frames = samples.reshape(inputs, samples.shape[2] // POINTS, POINTS)
    chans = CHANNELS // freq_size // 2
    voltages = channelize(frames, filter_table(chan_list, freq_size))
    voltages = voltages.reshape(2 * freq_size, 2, chans, inputs, SPECTRA)

    pair = lax.all_to_all(voltages, ("freq", "column"), split_axis=0, concat_axis=0, tiled=True)
    pair = pair.reshape(freq_size, 2, 2, chans, inputs, SPECTRA)
    pair = jnp.stack(
        [
            lax.dynamic_index_in_dim(pair, side, 1, keepdims=False).transpose(1, 2, 0, 3, 4)
            for side in (column, 1 - column)
        ],
        axis=1,
    )

    blocks, tiles = {0: pair.reshape(2, 2, chans, tile, SPECTRA)}, {}

    def near(*partners):
        sources = [blocks[0 if at == half else at] for at in partners]
        swaps = [
            jnp.bool_(True) if at == half else (plane + at) % half > plane for at in partners
        ]
        mine, theirs = visibilities(blocks[0], sources, swaps)
        moved = to_twin(theirs)
        for index, at in enumerate(partners):
            tiles[half if at == half else -at % half] = (mine[index], moved[index])

    def far(owner, partner):
        swap = (plane + partner) % half > (plane + owner) % half
        mine, theirs = visibilities(blocks[owner], [blocks[partner]], [swap])
        tiles[(owner - partner) % half] = (
            along_ring(mine, owner)[0],
            along_ring(theirs, owner, 1)[0],
        )

    def step(partner):
        way = 1 if partner < 0 else -1
        blocks[partner] = along_ring(blocks[partner + way], way)

    def settle():
        nonlocal tiles, blocks
        tiles, blocks = lax.optimization_barrier((tiles, blocks))

    step(-1), step(1)
    near(0, half)
    settle()
    step(-2), step(2)
    near(-1, 1)
    settle()
    step(-3)
    near(-2, 2)
    far(-1, 2)
    settle()
    far(1, -3)
    near(-3)

    def whole(place):
        return jnp.stack([tiles[offset][place] for offset in range(half + 1)], axis=1)

    mine, theirs = whole(0), whole(1)
    low = jnp.where(column == 0, mine, theirs)
    high = jnp.where(column == 0, theirs, mine)
    return jnp.concatenate([low, high], axis=0)[:, None]


def solution(mesh):
    freq_size, blk_size = mesh.devices.shape
    planes = Mesh(
        mesh.devices.reshape(freq_size, 2, blk_size // 2), ("freq", "column", "plane")
    )
    blk = ("column", "plane")
    in_specs = (P(blk, "freq", None), P())
    out_specs = P("freq", blk, None, None, None, None)
    return jax.shard_map(body, mesh=planes, in_specs=in_specs, out_specs=out_specs, check_vma=False)
```

```python
import jax
import jax.numpy as jnp
from jax import lax
from jax.experimental import pallas as pl
from jax.experimental.pallas import tpu as pltpu
from jax.sharding import Mesh
from jax.sharding import PartitionSpec as P

POINTS = 256
TAPS = 16
CHANNELS = 128
SPECTRA = 256


def along_ring(value, steps, other=0):
    half = lax.axis_size("plane")
    pairs = []
    for b in range(2 * half):
        column, plane = b // half, b % half
        pairs.append((b, (column + other) % 2 * half + (plane + steps) % half))
    return lax.ppermute(value, ("column", "plane"), pairs)


def to_twin(value):
    return along_ring(value, 0, 1)


def filter_table(chan_list, freq_size):
    window_len = TAPS * POINTS
    position = jnp.arange(window_len, dtype=jnp.float32)
    offset_pos = (position - window_len / 2 + 0.5) / POINTS
    taper = 0.5 - 0.5 * jnp.cos(2.0 * jnp.pi * (position + 0.5) / window_len)
    window = jnp.sin(jnp.pi * offset_pos) / (jnp.pi * offset_pos) * taper
    window = window / jnp.sqrt(jnp.sum(window * window))
    window = window.reshape(TAPS, 1, POINTS)
    columns = jnp.arange(POINTS, dtype=jnp.int32)
    angles = (chan_list[:, None] * columns[None, :] % POINTS).astype(jnp.float32) * (
        2.0 * jnp.pi / POINTS
    )
    waves = jnp.stack([jnp.cos(angles), -jnp.sin(angles)], axis=0)
    waves = waves.reshape(2, freq_size, 2, -1, POINTS).transpose(1, 2, 0, 3, 4)
    return (window * waves.reshape(1, -1, POINTS)).astype(jnp.bfloat16)


def channelize(frames, filters):
    return lax.conv_general_dilated(
        frames,
        filters,
        window_strides=(1,),
        padding="VALID",
        dimension_numbers=("NWC", "WOI", "CNW"),
        preferred_element_type=jnp.float32,
    ).astype(jnp.bfloat16)


def visibility_kernel(swaps, own, *refs):
    partners, (kept, given) = refs[:-2], refs[-2:]
    for chan in range(own.shape[2]):
        for block in range(2):
            real, imag = own[0, block, chan], own[1, block, chan]
            stacked = jnp.concatenate(
                [
                    jnp.concatenate([real, imag], axis=1),
                    jnp.concatenate([imag, -real], axis=1),
                ],
                axis=0,
            )
            tile = real.shape[0]
            found = kept if block == 0 else given
            for index, partner in enumerate(partners):
                other = swaps[index] if block == 0 else 1 - swaps[index]
                moving = jnp.concatenate([partner[0, other, chan], partner[1, other, chan]], axis=1)
                product = lax.dot_general(
                    stacked, moving, (((1,), (1,)), ((), ())), preferred_element_type=jnp.float32
                )
                product = (product * (1.0 / SPECTRA)).astype(jnp.bfloat16)
                found[index, chan, 0] = product[:tile]
                found[index, chan, 1] = product[tile:]


def visibilities(own, partners, swaps):
    _, _, chans, tile, spectra = own.shape
    count = len(partners)
    data = pl.BlockSpec((2, 2, 2, tile, spectra), lambda chan, _: (0, 0, chan, 0, 0))
    made = pl.BlockSpec((count, 2, 2, tile, tile), lambda chan, _: (0, chan, 0, 0, 0))
    shape = jax.ShapeDtypeStruct((count, chans, 2, tile, tile), jnp.bfloat16)
    return pl.pallas_call(
        visibility_kernel,
        grid_spec=pltpu.PrefetchScalarGridSpec(
            num_scalar_prefetch=1,
            grid=(chans // 2,),
            in_specs=[data] * (1 + count),
            out_specs=[made, made],
        ),
        out_shape=[shape, shape],
        compiler_params=pltpu.CompilerParams(vmem_limit_bytes=24 * 1024 * 1024),
    )(jnp.stack(swaps).astype(jnp.int32), own, *partners)


def placement_kernel(column, *refs):
    out, sources = refs[-1], refs[:6]
    side, part = pl.program_id(0), pl.program_id(1)
    local = side == column[0]
    for index in range(3):
        at = jnp.where(part == 0, index, 2 - index)

        @pl.when(local)
        def _(index=index, at=at):
            out[:, 0, at] = sources[2 * index][0]

        @pl.when(jnp.logical_not(local))
        def _(index=index, at=at):
            out[:, 0, at] = sources[2 * index + 1][0]


def placed(column, groups, parts, first, into=None):
    _, chans, two, tile, _ = groups[0][0].shape
    sources = [array for group in groups for array in group]
    source = pl.BlockSpec(
        (1, chans, two, tile, tile), lambda side, part, _: (part, 0, 0, 0, 0)
    )
    made = pl.BlockSpec(
        (chans, 1, 3, two, tile, tile), lambda side, part, _: (side, 0, first + 2 * part, 0, 0, 0)
    )
    kept = [] if into is None else [into]
    return pl.pallas_call(
        placement_kernel,
        grid_spec=pltpu.PrefetchScalarGridSpec(
            num_scalar_prefetch=1,
            grid=(2, parts),
            in_specs=[source] * 6 + [pl.BlockSpec(memory_space=pl.ANY)] * len(kept),
            out_specs=made,
        ),
        out_shape=jax.ShapeDtypeStruct((2 * chans, 1, 9, two, tile, tile), jnp.bfloat16),
        input_output_aliases={7: 0} if kept else {},
        compiler_params=pltpu.CompilerParams(vmem_limit_bytes=24 * 1024 * 1024),
    )(column.astype(jnp.int32)[None], *sources, *kept)


def body(samples, chan_list):
    freq_size = lax.axis_size("freq")
    half = lax.axis_size("plane")
    column, plane = lax.axis_index("column"), lax.axis_index("plane")
    inputs = samples.shape[1]
    tile = freq_size * inputs
    frames = samples.reshape(inputs, samples.shape[2] // POINTS, POINTS)
    chans = CHANNELS // freq_size // 2
    voltages = channelize(frames, filter_table(chan_list, freq_size))
    voltages = voltages.reshape(2 * freq_size, 2, chans, inputs, SPECTRA)

    pair = lax.all_to_all(voltages, ("freq", "column"), split_axis=0, concat_axis=0, tiled=True)
    pair = pair.reshape(freq_size, 2, 2, chans, inputs, SPECTRA)
    pair = jnp.stack(
        [
            lax.dynamic_index_in_dim(pair, side, 1, keepdims=False).transpose(1, 2, 0, 3, 4)
            for side in (column, 1 - column)
        ],
        axis=1,
    )

    blocks, tiles = {0: pair.reshape(2, 2, chans, tile, SPECTRA)}, {}

    def near(*partners):
        sources = [blocks[0 if at == half else at] for at in partners]
        swaps = [
            jnp.bool_(True) if at == half else (plane + at) % half > plane for at in partners
        ]
        mine, theirs = visibilities(blocks[0], sources, swaps)
        tiles[tuple(half if at == half else -at % half for at in partners)] = (
            mine,
            to_twin(theirs),
        )

    def far(owner, partner):
        swap = (plane + partner) % half > (plane + owner) % half
        mine, theirs = visibilities(blocks[owner], [blocks[partner]], [swap])
        tiles[((owner - partner) % half,)] = (
            along_ring(mine, owner),
            along_ring(theirs, owner, 1),
        )

    def step(partner):
        way = 1 if partner < 0 else -1
        blocks[partner] = along_ring(blocks[partner + way], way)

    def settle():
        nonlocal tiles, blocks
        tiles, blocks = lax.optimization_barrier((tiles, blocks))

    step(-1), step(1)
    near(0, half)
    settle()
    step(-2), step(2)
    near(-1, 1)
    settle()
    step(-3)
    near(-2, 2)
    far(-1, 2)
    settle()
    far(1, -3)
    near(-3)
    most = placed(column, [tiles[0, 8], tiles[1, 7], tiles[2, 6]], 2, 0)
    return placed(column, [tiles[(3,)], tiles[(4,)], tiles[(5,)]], 1, 1, most)


def solution(mesh):
    freq_size, blk_size = mesh.devices.shape
    planes = Mesh(
        mesh.devices.reshape(freq_size, 2, blk_size // 2), ("freq", "column", "plane")
    )
    blk = ("column", "plane")
    in_specs = (P(blk, "freq", None), P())
    out_specs = P("freq", blk, None, None, None, None)
    return jax.shard_map(body, mesh=planes, in_specs=in_specs, out_specs=out_specs, check_vma=False)
```

```python
import jax
import jax.numpy as jnp
from jax import lax
from jax.experimental import pallas as pl
from jax.experimental.pallas import tpu as pltpu
from jax.sharding import Mesh
from jax.sharding import PartitionSpec as P

POINTS = 256
TAPS = 16
CHANNELS = 128
SPECTRA = 256


def along_ring(value, steps, other=0):
    half = lax.axis_size("plane")
    pairs = []
    for b in range(2 * half):
        column, plane = b // half, b % half
        pairs.append((b, (column + other) % 2 * half + (plane + steps) % half))
    return lax.ppermute(value, ("column", "plane"), pairs)


def to_twin(value):
    return along_ring(value, 0, 1)


def filter_table(chan_list, freq_size):
    window_len = TAPS * POINTS
    position = jnp.arange(window_len, dtype=jnp.float32)
    offset_pos = (position - window_len / 2 + 0.5) / POINTS
    taper = 0.5 - 0.5 * jnp.cos(2.0 * jnp.pi * (position + 0.5) / window_len)
    window = jnp.sin(jnp.pi * offset_pos) / (jnp.pi * offset_pos) * taper
    window = window / jnp.sqrt(jnp.sum(window * window))
    window = window.reshape(TAPS, 1, POINTS)
    columns = jnp.arange(POINTS, dtype=jnp.int32)
    angles = (chan_list[:, None] * columns[None, :] % POINTS).astype(jnp.float32) * (
        2.0 * jnp.pi / POINTS
    )
    waves = jnp.stack([jnp.cos(angles), -jnp.sin(angles)], axis=0)
    waves = waves.reshape(2, freq_size, 2, -1, POINTS).transpose(1, 2, 0, 3, 4)
    return (window * waves.reshape(1, -1, POINTS)).astype(jnp.bfloat16)


def channelize(frames, filters):
    return lax.conv_general_dilated(
        frames,
        filters,
        window_strides=(1,),
        padding="VALID",
        dimension_numbers=("NWC", "WOI", "CNW"),
        preferred_element_type=jnp.float32,
    ).astype(jnp.bfloat16)


def visibility_kernel(places, own, *refs):
    partners, found = refs[:-1], refs[-1]
    for chan in range(own.shape[2]):
        real, imag = own[0, 0, chan], own[1, 0, chan]
        stacked = jnp.concatenate(
            [
                jnp.concatenate([real, imag], axis=1),
                jnp.concatenate([imag, -real], axis=1),
            ],
            axis=0,
        )
        tile = real.shape[0]
        for index, partner in enumerate(partners):
            moving = jnp.concatenate([partner[0, 0, chan], partner[1, 0, chan]], axis=1)
            product = lax.dot_general(
                stacked, moving, (((1,), (1,)), ((), ())), preferred_element_type=jnp.float32
            )
            product = (product * (1.0 / SPECTRA)).astype(jnp.bfloat16)
            found[index, chan, 0] = product[:tile]
            found[index, chan, 1] = product[tile:]


def visibilities(own, partners, swaps, block):
    _, _, chans, tile, spectra = own.shape
    count = len(partners)
    shape = (2, 1, 2, tile, spectra)
    places = jnp.stack(swaps).astype(jnp.int32) ^ block
    return pl.pallas_call(
        visibility_kernel,
        grid_spec=pltpu.PrefetchScalarGridSpec(
            num_scalar_prefetch=1,
            grid=(chans // 2,),
            in_specs=[pl.BlockSpec(shape, lambda chan, _: (0, block, chan, 0, 0))]
            + [
                pl.BlockSpec(shape, lambda chan, at, index=index: (0, at[index], chan, 0, 0))
                for index in range(count)
            ],
            out_specs=pl.BlockSpec((count, 2, 2, tile, tile), lambda chan, _: (0, chan, 0, 0, 0)),
        ),
        out_shape=jax.ShapeDtypeStruct((count, chans, 2, tile, tile), jnp.bfloat16),
        compiler_params=pltpu.CompilerParams(vmem_limit_bytes=24 * 1024 * 1024),
    )(places, own, *partners)


def placement_kernel(column, *refs):
    out, sources = refs[-1], refs[:6]
    side, part = pl.program_id(0), pl.program_id(1)
    local = side == column[0]
    for index in range(3):
        at = jnp.where(part == 0, index, 2 - index)

        @pl.when(local)
        def _(index=index, at=at):
            out[:, 0, at] = sources[2 * index][0]

        @pl.when(jnp.logical_not(local))
        def _(index=index, at=at):
            out[:, 0, at] = sources[2 * index + 1][0]


def placed(column, groups, parts, first, into=None):
    _, chans, two, tile, _ = groups[0][0].shape
    sources = [array for group in groups for array in group]
    source = pl.BlockSpec(
        (1, chans, two, tile, tile), lambda side, part, _: (part, 0, 0, 0, 0)
    )
    made = pl.BlockSpec(
        (chans, 1, 3, two, tile, tile), lambda side, part, _: (side, 0, first + 2 * part, 0, 0, 0)
    )
    kept = [] if into is None else [into]
    return pl.pallas_call(
        placement_kernel,
        grid_spec=pltpu.PrefetchScalarGridSpec(
            num_scalar_prefetch=1,
            grid=(2, parts),
            in_specs=[source] * 6 + [pl.BlockSpec(memory_space=pl.ANY)] * len(kept),
            out_specs=made,
        ),
        out_shape=jax.ShapeDtypeStruct((2 * chans, 1, 9, two, tile, tile), jnp.bfloat16),
        input_output_aliases={7: 0} if kept else {},
        compiler_params=pltpu.CompilerParams(vmem_limit_bytes=24 * 1024 * 1024),
    )(column.astype(jnp.int32)[None], *sources, *kept)


def body(samples, chan_list):
    freq_size = lax.axis_size("freq")
    half = lax.axis_size("plane")
    column, plane = lax.axis_index("column"), lax.axis_index("plane")
    inputs = samples.shape[1]
    tile = freq_size * inputs
    frames = samples.reshape(inputs, samples.shape[2] // POINTS, POINTS)
    chans = CHANNELS // freq_size // 2
    voltages = channelize(frames, filter_table(chan_list, freq_size))
    voltages = voltages.reshape(2 * freq_size, 2, chans, inputs, SPECTRA)

    pair = lax.all_to_all(voltages, ("freq", "column"), split_axis=0, concat_axis=0, tiled=True)
    pair = pair.reshape(freq_size, 2, 2, chans, inputs, SPECTRA)
    pair = jnp.stack(
        [
            lax.dynamic_index_in_dim(pair, side, 1, keepdims=False).transpose(1, 2, 0, 3, 4)
            for side in (column, 1 - column)
        ],
        axis=1,
    )

    blocks, tiles = {0: pair.reshape(2, 2, chans, tile, SPECTRA)}, {}

    def near(*partners):
        sources = [blocks[0 if at == half else at] for at in partners]
        swaps = [
            jnp.bool_(True) if at == half else (plane + at) % half > plane for at in partners
        ]
        theirs = visibilities(blocks[0], sources, swaps, 1)
        mine = visibilities(blocks[0], sources, swaps, 0)
        tiles[tuple(half if at == half else -at % half for at in partners)] = (
            mine,
            to_twin(theirs),
        )

    def far(owner, partner):
        swap = (plane + partner) % half > (plane + owner) % half
        theirs = visibilities(blocks[owner], [blocks[partner]], [swap], 1)
        mine = visibilities(blocks[owner], [blocks[partner]], [swap], 0)
        tiles[((owner - partner) % half,)] = (
            along_ring(mine, owner),
            along_ring(theirs, owner, 1),
        )

    def step(partner):
        way = 1 if partner < 0 else -1
        blocks[partner] = along_ring(blocks[partner + way], way)

    def settle():
        nonlocal tiles, blocks
        tiles, blocks = lax.optimization_barrier((tiles, blocks))

    step(-1), step(1)
    near(0, half)
    settle()
    step(-2), step(2)
    near(-1, 1)
    settle()
    step(-3)
    near(-2, 2)
    far(-1, 2)
    settle()
    far(1, -3)
    near(-3)
    most = placed(column, [tiles[0, 8], tiles[1, 7], tiles[2, 6]], 2, 0)
    return placed(column, [tiles[(3,)], tiles[(4,)], tiles[(5,)]], 1, 1, most)


def solution(mesh):
    freq_size, blk_size = mesh.devices.shape
    planes = Mesh(
        mesh.devices.reshape(freq_size, 2, blk_size // 2), ("freq", "column", "plane")
    )
    blk = ("column", "plane")
    in_specs = (P(blk, "freq", None), P())
    out_specs = P("freq", blk, None, None, None, None)
    return jax.shard_map(body, mesh=planes, in_specs=in_specs, out_specs=out_specs, check_vma=False)
```

```python
import jax
import jax.numpy as jnp
from jax import lax
from jax.experimental import pallas as pl
from jax.experimental.pallas import tpu as pltpu
from jax.sharding import Mesh
from jax.sharding import PartitionSpec as P

POINTS = 256
TAPS = 16
CHANNELS = 128
SPECTRA = 256


def along_ring(value, steps, other=0):
    half = lax.axis_size("plane")
    pairs = []
    for b in range(2 * half):
        column, plane = b // half, b % half
        pairs.append((b, (column + other) % 2 * half + (plane + steps) % half))
    return lax.ppermute(value, ("column", "plane"), pairs)


def to_twin(value):
    return along_ring(value, 0, 1)


def filter_table(chan_list, freq_size):
    window_len = TAPS * POINTS
    position = jnp.arange(window_len, dtype=jnp.float32)
    offset_pos = (position - window_len / 2 + 0.5) / POINTS
    taper = 0.5 - 0.5 * jnp.cos(2.0 * jnp.pi * (position + 0.5) / window_len)
    window = jnp.sin(jnp.pi * offset_pos) / (jnp.pi * offset_pos) * taper
    window = window / jnp.sqrt(jnp.sum(window * window))
    window = window.reshape(TAPS, 1, POINTS)
    columns = jnp.arange(POINTS, dtype=jnp.int32)
    angles = (chan_list[:, None] * columns[None, :] % POINTS).astype(jnp.float32) * (
        2.0 * jnp.pi / POINTS
    )
    waves = jnp.stack([jnp.cos(angles), -jnp.sin(angles)], axis=0)
    waves = waves.reshape(2, freq_size, 2, -1, POINTS).transpose(1, 2, 0, 3, 4)
    return (window * waves.reshape(1, -1, POINTS)).astype(jnp.bfloat16)


def channelize(frames, filters):
    return lax.conv_general_dilated(
        frames,
        filters,
        window_strides=(1,),
        padding="VALID",
        dimension_numbers=("NWC", "WOI", "CNW"),
        preferred_element_type=jnp.float32,
    ).astype(jnp.bfloat16)


def visibility_kernel(places, own, *refs):
    partners, found = refs[:-1], refs[-1]
    for chan in range(own.shape[2]):
        real, imag = own[0, 0, chan], own[1, 0, chan]
        stacked = jnp.concatenate(
            [
                jnp.concatenate([real, imag], axis=1),
                jnp.concatenate([imag, -real], axis=1),
            ],
            axis=0,
        )
        tile = real.shape[0]
        for index, partner in enumerate(partners):
            moving = jnp.concatenate([partner[0, 0, chan], partner[1, 0, chan]], axis=1)
            product = lax.dot_general(
                stacked, moving, (((1,), (1,)), ((), ())), preferred_element_type=jnp.float32
            )
            product = (product * (1.0 / SPECTRA)).astype(jnp.bfloat16)
            found[index, chan, 0] = product[:tile]
            found[index, chan, 1] = product[tile:]


def visibilities(own, partners, swaps, block):
    _, _, chans, tile, spectra = own.shape
    count = len(partners)
    shape = (2, 1, chans, tile, spectra)
    places = jnp.stack(swaps).astype(jnp.int32) ^ block
    return pl.pallas_call(
        visibility_kernel,
        grid_spec=pltpu.PrefetchScalarGridSpec(
            num_scalar_prefetch=1,
            grid=(1,),
            in_specs=[pl.BlockSpec(shape, lambda chan, _: (0, block, chan, 0, 0))]
            + [
                pl.BlockSpec(shape, lambda chan, at, index=index: (0, at[index], chan, 0, 0))
                for index in range(count)
            ],
            out_specs=pl.BlockSpec((count, chans, 2, tile, tile), lambda chan, _: (0, chan, 0, 0, 0)),
        ),
        out_shape=jax.ShapeDtypeStruct((count, chans, 2, tile, tile), jnp.bfloat16),
        compiler_params=pltpu.CompilerParams(vmem_limit_bytes=24 * 1024 * 1024),
    )(places, own, *partners)


def placement_kernel(column, *refs):
    out, sources = refs[-1], refs[:6]
    side, part = pl.program_id(0), pl.program_id(1)
    local = side == column[0]
    for index in range(3):
        at = jnp.where(part == 0, index, 2 - index)

        @pl.when(local)
        def _(index=index, at=at):
            out[:, 0, at] = sources[2 * index][0]

        @pl.when(jnp.logical_not(local))
        def _(index=index, at=at):
            out[:, 0, at] = sources[2 * index + 1][0]


def placed(column, groups, parts, first, into=None):
    _, chans, two, tile, _ = groups[0][0].shape
    sources = [array for group in groups for array in group]
    source = pl.BlockSpec(
        (1, chans, two, tile, tile), lambda side, part, _: (part, 0, 0, 0, 0)
    )
    made = pl.BlockSpec(
        (chans, 1, 3, two, tile, tile), lambda side, part, _: (side, 0, first + 2 * part, 0, 0, 0)
    )
    kept = [] if into is None else [into]
    return pl.pallas_call(
        placement_kernel,
        grid_spec=pltpu.PrefetchScalarGridSpec(
            num_scalar_prefetch=1,
            grid=(2, parts),
            in_specs=[source] * 6 + [pl.BlockSpec(memory_space=pl.ANY)] * len(kept),
            out_specs=made,
        ),
        out_shape=jax.ShapeDtypeStruct((2 * chans, 1, 9, two, tile, tile), jnp.bfloat16),
        input_output_aliases={7: 0} if kept else {},
        compiler_params=pltpu.CompilerParams(vmem_limit_bytes=24 * 1024 * 1024),
    )(column.astype(jnp.int32)[None], *sources, *kept)


def body(samples, chan_list):
    freq_size = lax.axis_size("freq")
    half = lax.axis_size("plane")
    column, plane = lax.axis_index("column"), lax.axis_index("plane")
    inputs = samples.shape[1]
    tile = freq_size * inputs
    frames = samples.reshape(inputs, samples.shape[2] // POINTS, POINTS)
    chans = CHANNELS // freq_size // 2
    voltages = channelize(frames, filter_table(chan_list, freq_size))
    voltages = voltages.reshape(2 * freq_size, 2, chans, inputs, SPECTRA)

    pair = lax.all_to_all(voltages, ("freq", "column"), split_axis=0, concat_axis=0, tiled=True)
    pair = pair.reshape(freq_size, 2, 2, chans, inputs, SPECTRA)
    pair = jnp.stack(
        [
            lax.dynamic_index_in_dim(pair, side, 1, keepdims=False).transpose(1, 2, 0, 3, 4)
            for side in (column, 1 - column)
        ],
        axis=1,
    )

    blocks, tiles = {0: pair.reshape(2, 2, chans, tile, SPECTRA)}, {}

    def near(*partners):
        sources = [blocks[0 if at == half else at] for at in partners]
        swaps = [
            jnp.bool_(True) if at == half else (plane + at) % half > plane for at in partners
        ]
        theirs = visibilities(blocks[0], sources, swaps, 1)
        mine = visibilities(blocks[0], sources, swaps, 0)
        tiles[tuple(half if at == half else -at % half for at in partners)] = (
            mine,
            to_twin(theirs),
        )

    def far(owner, partner):
        swap = (plane + partner) % half > (plane + owner) % half
        theirs = visibilities(blocks[owner], [blocks[partner]], [swap], 1)
        mine = visibilities(blocks[owner], [blocks[partner]], [swap], 0)
        tiles[((owner - partner) % half,)] = (
            along_ring(mine, owner),
            along_ring(theirs, owner, 1),
        )

    def step(partner):
        way = 1 if partner < 0 else -1
        blocks[partner] = along_ring(blocks[partner + way], way)

    def settle():
        nonlocal tiles, blocks
        tiles, blocks = lax.optimization_barrier((tiles, blocks))

    step(-1), step(1)
    near(0, half)
    settle()
    step(-2), step(2)
    near(-1, 1)
    settle()
    step(-3)
    near(-2, 2)
    far(-1, 2)
    settle()
    far(1, -3)
    near(-3)
    most = placed(column, [tiles[0, 8], tiles[1, 7], tiles[2, 6]], 2, 0)
    return placed(column, [tiles[(3,)], tiles[(4,)], tiles[(5,)]], 1, 1, most)


def solution(mesh):
    freq_size, blk_size = mesh.devices.shape
    planes = Mesh(
        mesh.devices.reshape(freq_size, 2, blk_size // 2), ("freq", "column", "plane")
    )
    blk = ("column", "plane")
    in_specs = (P(blk, "freq", None), P())
    out_specs = P("freq", blk, None, None, None, None)
    return jax.shard_map(body, mesh=planes, in_specs=in_specs, out_specs=out_specs, check_vma=False)
```
